32 devices in a mesh: section: 2 (over core), ctx: 4 (over y, x), wshard: 4 (over z).
Axes of the slice: x: 2, y: 2, z: 4, core: 2. Of those that a mesh axis runs over, the one named last changes fastest.
Arguments:
- tokens: bfloat16 [8, 1024, 768], P('wshard', 'ctx'), may hold values from -6 to 6
- cotangent: bfloat16 [8, 1024, 768], P('wshard', 'ctx'), may hold values from -6 to 6
- block_map: int32 [8, 8], P('wshard'), may hold values from 0 to 7, each once within a row
- w_qkv: bfloat16 [2, 768, 2304], P('section', 'wshard'), may hold values from -0.21875 to 0.21875
- b_qkv: bfloat16 [2, 2304], P('section', 'wshard'), may hold values from -3 to 3
- w_out: bfloat16 [2, 768, 768], P('section', 'wshard'), may hold values from -1.75 to 1.75
- b_out: bfloat16 [2, 768], P('section', 'wshard'), may hold values from -3 to 3
- w_up: bfloat16 [2, 768, 3072], P('section', 'wshard'), may hold values from -0.21875 to 0.21875
- b_up: bfloat16 [2, 3072], P('section', 'wshard'), may hold values from -3 to 3
- w_down: bfloat16 [2, 3072, 768], P('section', 'wshard'), may hold values from -0.109375 to 0.109375
- b_down: bfloat16 [2, 768], P('section', 'wshard'), may hold values from -3 to 3
- gain_attn: bfloat16 [2, 768], P('section', 'wshard'), may hold values from 0.5 to 1.5
- shift_attn: bfloat16 [2, 768], P('section', 'wshard'), may hold values from -2 to 2
- gain_mlp: bfloat16 [2, 768], P('section', 'wshard'), may hold values from 0.5 to 1.5
- shift_mlp: bfloat16 [2, 768], P('section', 'wshard'), may hold values from -2 to 2
Outputs:
- layer_outputs: bfloat16 [2, 8, 1024, 768], P('section', 'wshard', 'ctx')
- boundary_grads: float32 [2, 8, 1024, 768], P('section', 'wshard', 'ctx')
- grad_w_qkv: float32 [2, 768, 2304], P('section', 'wshard')
- grad_b_qkv: float32 [2, 2304], P('section', 'wshard')
- grad_w_out: float32 [2, 768, 768], P('section', 'wshard')
- grad_b_out: float32 [2, 768], P('section', 'wshard')
- grad_w_up: float32 [2, 768, 3072], P('section', 'wshard')
- grad_b_up: float32 [2, 3072], P('section', 'wshard')
- grad_w_down: float32 [2, 3072, 768], P('section', 'wshard')
- grad_b_down: float32 [2, 768], P('section', 'wshard')
- grad_gain_attn: float32 [2, 768], P('section', 'wshard')
- grad_shift_attn: float32 [2, 768], P('section', 'wshard')
- grad_gain_mlp: float32 [2, 768], P('section', 'wshard')
- grad_shift_mlp: float32 [2, 768], P('section', 'wshard')
The draws below stay inside these ranges and needn't reach their ends.
Inputs may be any that keep to these rules, and one draw needn't show every extreme that they name: Each row is an order of the 8 blocks of 128 tokens of one sequence: stored slot i holds block block_map[s, i], and each block stands in one slot.
All inputs are finite; a program needn't handle non-finite values.
Results may differ from the reference program's by a relative error of at most 0.015.
Values may be sent and summed in bfloat16 or wider, within the bound.
A program may use at most 320 MiB of HBM per device.

```python
import math
import jax
import jax.numpy as jnp
from jax import lax

D = 768
H = 12
HD = 64
FF = 3072
ROT = 16
SEQLEN = 1024
NBLK = 8
SEQS = 8


def shard_levels(key, extent, shards, low, top_value):
    loudness, own = 1.0, jax.random.fold_in(key, 6)
    for position, shards_of in shards:
        heights = jnp.exp(jax.random.uniform(jax.random.fold_in(own, position), (shards_of,), jnp.float32, low / len(shards), top_value / len(shards)))
        loudness = loudness * jnp.repeat(heights, extent[position] // shards_of).reshape([-1 if axis == position else 1 for axis in range(len(extent))])
    return loudness


def bell_draw(key, extent, scale, bound, pieces=(), kind=jnp.bfloat16):
    drawn = jax.random.normal(key, extent, jnp.float32) * scale
    if len(pieces) > 0:
        drawn = shard_levels(key, extent, pieces, -0.22, 0.18) * drawn
    return jnp.clip(drawn, min=-bound, max=bound).astype(kind)


def setup_inputs(seed: int = 0) -> dict:
    key_list = jax.random.split(jax.random.key(seed), 16)
    tokens = bell_draw(key_list[0], (SEQS, SEQLEN, D), 1.0, 6.0, ((0, 4), (1, 4)))
    cotangent = bell_draw(key_list[1], (SEQS, SEQLEN, D), 1.0, 6.0, ((0, 4), (1, 4)))
    block_map = jax.vmap(lambda own: jax.random.permutation(own, NBLK))(jax.random.split(key_list[2], SEQS)).reshape((SEQS, NBLK)).astype(jnp.int32)
    w_qkv = bell_draw(key_list[3], (2, D, 3 * D), D ** -0.5, 0.21875, ((0, 2), (1, 4)))
    b_qkv = bell_draw(key_list[4], (2, 3 * D), 0.5, 3.0, ((0, 2), (1, 4)))
    w_out = bell_draw(key_list[5], (2, D, D), (max(D // 64, 1)) ** -0.5, 1.75, ((0, 2), (1, 4)))
    b_out = bell_draw(key_list[6], (2, D), 0.5, 3.0, ((0, 2), (1, 4)))
    w_up = bell_draw(key_list[7], (2, D, FF), D ** -0.5, 0.21875, ((0, 2), (1, 4)))
    b_up = bell_draw(key_list[8], (2, FF), 0.5, 3.0, ((0, 2), (1, 4)))
    w_down = bell_draw(key_list[9], (2, FF, D), FF ** -0.5, 0.109375, ((0, 2), (1, 4)))
    b_down = bell_draw(key_list[10], (2, D), 0.5, 3.0, ((0, 2), (1, 4)))
    gain_attn = jnp.clip(1.0 + 0.1 * jax.random.normal(key_list[11], (2, D), jnp.float32), 0.5, 1.5).astype(jnp.bfloat16)
    shift_attn = bell_draw(key_list[12], (2, D), 0.3, 2.0, ((0, 2), (1, 4)))
    gain_mlp = jnp.clip(1.0 + 0.1 * jax.random.normal(key_list[13], (2, D), jnp.float32), 0.5, 1.5).astype(jnp.bfloat16)
    shift_mlp = bell_draw(key_list[14], (2, D), 0.3, 2.0, ((0, 2), (1, 4)))
    return {"tokens": tokens, "cotangent": cotangent, "block_map": block_map, "w_qkv": w_qkv, "b_qkv": b_qkv, "w_out": w_out, "b_out": b_out, "w_up": w_up, "b_up": b_up, "w_down": w_down, "b_down": b_down, "gain_attn": gain_attn, "shift_attn": shift_attn, "gain_mlp": gain_mlp, "shift_mlp": shift_mlp}


@jax.custom_vjp
def low(v):
    return lax.optimization_barrier(v.astype(jnp.bfloat16)).astype(jnp.float32)

@jax.custom_vjp
def low_back(v):
    return v

def low_keep(v):
    return (low(v), None)

def low_pass(kept, grad):
    return (grad,)

def back_keep(v):
    return (v, None)

def back_low(kept, grad):
    return (low(grad),)
low.defvjp(low_keep, low_pass)
low_back.defvjp(back_keep, back_low)
EPSILON = 1e-05
HIGHEST = lax.Precision.HIGHEST

def layer_norm(values, gain_vec, shift_vec):
    center = values - lax.optimization_barrier(jnp.mean(values, axis=-1, keepdims=True))
    spread = lax.optimization_barrier(jnp.mean(center * center, axis=-1, keepdims=True))
    return center * lax.rsqrt(spread + EPSILON) * gain_vec + shift_vec

def angles(places, rot_width):
    half_width = rot_width // 2
    frequency = jnp.exp(jnp.arange(half_width, dtype=jnp.float32) * jnp.float32(-2.0 * math.log(10000.0) / rot_width))
    return places.astype(jnp.float32)[:, None] * frequency[None, :]

def rotate(tensor, turn_angle, rotation_sign):
    half_width = turn_angle.shape[-1]
    cosine = jnp.cos(turn_angle)[:, None, :]
    sine_term = rotation_sign * jnp.sin(turn_angle)[:, None, :]
    lower_half = tensor[..., :half_width]
    upper_half = tensor[..., half_width:2 * half_width]
    return jnp.concatenate([lower_half * cosine - upper_half * sine_term, upper_half * cosine + lower_half * sine_term, tensor[..., 2 * half_width:]], axis=-1)

def positions(order_row, block_rows):
    return jnp.repeat(order_row, block_rows) * block_rows + jnp.tile(jnp.arange(block_rows, dtype=jnp.int32), order_row.shape[0])

def matmul(left, right):
    return jnp.dot(left, right, precision=HIGHEST)

def layer(current, params, places):
    w_qkv, b_qkv, w_out, b_out, w_up, b_up, w_down, b_down, gain_attn, shift_attn, gain_mlp, shift_mlp = params
    current = low_back(current)
    row_count = current.shape[0]
    normed_a = low(layer_norm(current, gain_attn, shift_attn))
    normed_m = low(layer_norm(current, gain_mlp, shift_mlp))
    projected = low_back(matmul(normed_a, w_qkv) + b_qkv)
    turn_angle = angles(places, ROT)
    queries = low_back(low(rotate(projected[:, :D].reshape(row_count, H, HD), turn_angle, 1.0)))
    key_rows = low_back(low(rotate(projected[:, D:2 * D].reshape(row_count, H, HD), turn_angle, 1.0)))
    value_rows = low_back(low(projected[:, 2 * D:].reshape(row_count, H, HD)))
    scores = low_back(jnp.einsum('qhd,khd->hqk', queries, key_rows, precision=HIGHEST) * 0.125)
    visible = places[None, :] <= places[:, None]
    attn_probs = low(jax.nn.softmax(jnp.where(visible[None], scores, -1e+30), axis=-1))
    mixed_heads = low_back(low(jnp.einsum('hqk,khd->qhd', attn_probs, value_rows, precision=HIGHEST).reshape(row_count, D)))
    attn_branch = low_back(matmul(mixed_heads, w_out) + b_out)
    pre_act = low_back(matmul(normed_m, w_up) + b_up)
    active = low(jax.nn.gelu(pre_act, approximate=False))
    mlp_branch = low_back(matmul(active, w_down) + b_down)
    return low(current + attn_branch + mlp_branch)

def reference(tokens, cotangent, block_map, w_qkv, b_qkv, w_out, b_out, w_up, b_up, w_down, b_down, gain_attn, shift_attn, gain_mlp, shift_mlp):
    params = tuple((weight_arr.astype(jnp.float32) for weight_arr in (w_qkv, b_qkv, w_out, b_out, w_up, b_up, w_down, b_down, gain_attn, shift_attn, gain_mlp, shift_mlp)))
    lower_params = tuple((weight_arr[0] for weight_arr in params))
    upper_params = tuple((weight_arr[1] for weight_arr in params))
    block_rows = SEQLEN // NBLK

    def one_sequence(carry, element):
        sequence, grad_top, order_row = element
        places = positions(order_row.astype(jnp.int32), block_rows)

        def run_layer(values, weights):
            return layer(values, weights, places)
        middle, back_lower = jax.vjp(run_layer, sequence.astype(jnp.float32), lower_params)
        final, back_upper = jax.vjp(run_layer, middle, upper_params)
        grad_middle, grads_upper = back_upper(grad_top.astype(jnp.float32))
        grad_input, grads_lower = back_lower(grad_middle)
        carry = tuple((total + jnp.stack([first_term, second_term]) for total, first_term, second_term in zip(carry, grads_lower, grads_upper)))
        return (carry, (jnp.stack([middle, final]).astype(jnp.bfloat16), jnp.stack([grad_input, grad_middle])))
    start = tuple((jnp.zeros_like(weight_arr) for weight_arr in params))
    totals, (outputs, grads) = lax.scan(one_sequence, start, (tokens, cotangent, block_map))
    outputs = jnp.transpose(outputs, (1, 0, 2, 3))
    grads = jnp.transpose(grads, (1, 0, 2, 3))
    return (outputs, grads, totals[0], totals[1], totals[2], totals[3], totals[4], totals[5], totals[6], totals[7], totals[8], totals[9], totals[10], totals[11])
```

```python
import math

import jax
import jax.numpy as jnp
from jax import lax
from jax.experimental import pallas as pl
from jax.experimental.pallas import tpu as pltpu
from jax.sharding import PartitionSpec as P

D = 768
H = 12
HD = 64
FF = 3072
ROT = 16
EPSILON = 1e-05
F32 = jnp.float32
BF16 = jnp.bfloat16
PAIRS = H * HD // 128
VMEM_LIMIT = 48 * 1024 * 1024


def dot_t(left, right):
    return lax.dot_general(left, right, (((1,), (1,)), ((), ())), preferred_element_type=F32)


def t_dot(left, right):
    return lax.dot_general(left, right, (((0,), (0,)), ((), ())), preferred_element_type=F32)


def dot(left, right):
    return jnp.dot(left, right, preferred_element_type=F32)


def swapped(part):
    return lax.ppermute(part, "section", [(0, 1), (1, 0)])


def positions(order_row, block_rows):
    return jnp.repeat(order_row, block_rows) * block_rows + jnp.tile(
        jnp.arange(block_rows, dtype=jnp.int32), order_row.shape[0]
    )


def turn_tables(places):
    half = ROT // 2
    frequency = jnp.exp(
        jnp.arange(half, dtype=F32) * F32(-2.0 * math.log(10000.0) / ROT)
    )
    angle = places.astype(F32)[:, None] * frequency[None, :]
    cosine, sine = jnp.cos(angle), jnp.sin(angle)
    rows = places.shape[0]
    ones = jnp.ones((rows, HD - ROT), F32)
    blank = jnp.zeros((rows, HD - half), F32)
    gap = jnp.zeros((rows, half), F32)
    tail = jnp.zeros((rows, HD - ROT), F32)
    cos_head = jnp.concatenate([cosine, cosine, ones], axis=1)
    low_head = jnp.concatenate([-sine, blank], axis=1)
    high_head = jnp.concatenate([gap, sine, tail], axis=1)
    return tuple(
        jnp.concatenate([table, table], axis=1) for table in (cos_head, low_head, high_head)
    )


def turned(values, cos_t, low_t, high_t, sign):
    half = ROT // 2
    ahead = pltpu.roll(values, 128 - half, 1)
    behind = pltpu.roll(values, half, 1)
    return values * cos_t + sign * (ahead * low_t + behind * high_t)


def rotate_kernel(k_ref, v_ref, cos_ref, low_ref, high_ref, out_ref):
    out_ref[0] = turned(k_ref[...], cos_ref[...], low_ref[...], high_ref[...], 1.0).astype(BF16)
    out_ref[1] = v_ref[...].astype(BF16)


def rotate_keys(projected_kv, tables):
    rows = projected_kv.shape[0]
    table = pl.BlockSpec((rows, 128), lambda h: (0, 0))
    return pl.pallas_call(
        rotate_kernel,
        grid=(PAIRS,),
        in_specs=[
            pl.BlockSpec((rows, 128), lambda h: (0, h)),
            pl.BlockSpec((rows, 128), lambda h: (0, PAIRS + h)),
            table,
            table,
            table,
        ],
        out_specs=pl.BlockSpec((2, rows, 128), lambda h: (0, 0, h)),
        out_shape=jax.ShapeDtypeStruct((2, rows, D), BF16),
        compiler_params=pltpu.CompilerParams(vmem_limit_bytes=VMEM_LIMIT),
        name="rotate_keys",
    )(projected_kv, projected_kv, *tables)


def attend_kernel(
    q_ref, kv_ref, cos_ref, low_ref, high_ref, all_ref, own_ref, mixed_ref, query_ref, stat_ref
):
    query = turned(q_ref[...], cos_ref[...], low_ref[...], high_ref[...], 1.0).astype(BF16)
    query_ref[...] = query
    visible = all_ref[...] <= own_ref[...]
    outs = []
    for head in range(2):
        lanes = slice(head * HD, (head + 1) * HD)
        keys, values = kv_ref[0, :, lanes], kv_ref[1, :, lanes]
        scores = jnp.where(visible, dot_t(keys, query[:, lanes]) * 0.125, -1e30)
        top = jnp.max(scores, axis=0, keepdims=True)
        weights = jnp.exp(scores - top)
        total = jnp.sum(weights, axis=0, keepdims=True)
        probs = (weights * (1.0 / total)).astype(BF16)
        outs.append(t_dot(values, probs))
        stat_ref[0, head : head + 1, :] = top + jnp.log(total)
    mixed_ref[...] = jnp.concatenate(outs, axis=0).T.astype(BF16)


def attend(projected_q, key_values, own_tables, places_all, places_own):
    rows, total = projected_q.shape[0], key_values.shape[1]
    table = pl.BlockSpec((rows, 128), lambda h: (0, 0))
    block = pl.BlockSpec((rows, 128), lambda h: (0, h))
    return pl.pallas_call(
        attend_kernel,
        grid=(PAIRS,),
        in_specs=[
            block,
            pl.BlockSpec((2, total, 128), lambda h: (0, 0, h)),
            table,
            table,
            table,
            pl.BlockSpec((total, 1), lambda h: (0, 0)),
            pl.BlockSpec((1, rows), lambda h: (0, 0)),
        ],
        out_specs=[block, block, pl.BlockSpec((1, 2, rows), lambda h: (h, 0, 0))],
        out_shape=[
            jax.ShapeDtypeStruct((rows, D), BF16),
            jax.ShapeDtypeStruct((rows, D), BF16),
            jax.ShapeDtypeStruct((PAIRS, 2, rows), F32),
        ],
        compiler_params=pltpu.CompilerParams(vmem_limit_bytes=VMEM_LIMIT),
        name="attend",
        cost_estimate=pl.CostEstimate(
            flops=4 * rows * total * D * 2, bytes_accessed=8 * total * D, transcendentals=rows * total * H
        ),
    )(projected_q, key_values, *own_tables, places_all[:, None], places_own[None, :])


def attend_back_kernel(
    query_ref, kv_ref, grad_ref, stat_ref,
    cos_ref, low_ref, high_ref, cos_all_ref, low_all_ref, high_all_ref,
    all_ref, own_ref, gq_ref, gkv_ref,
):
    visible = all_ref[...] <= own_ref[...]
    gq, gk, gv = [], [], []
    for head in range(2):
        lanes = slice(head * HD, (head + 1) * HD)
        keys, values = kv_ref[0, :, lanes], kv_ref[1, :, lanes]
        query, grad = query_ref[:, lanes], grad_ref[:, lanes]
        scores = dot_t(keys, query) * 0.125
        probs = jnp.where(visible, jnp.exp(scores - stat_ref[0, head : head + 1, :]), 0.0)
        grad_probs = dot_t(values, grad)
        delta = jnp.sum(probs * grad_probs, axis=0, keepdims=True)
        grad_scores = (probs * (grad_probs - delta)).astype(BF16)
        gq.append(t_dot(keys, grad_scores))
        gk.append(dot(grad_scores, query))
        gv.append(dot(probs.astype(BF16), grad))
    grad_query = (jnp.concatenate(gq, axis=0).T * 0.125).astype(BF16).astype(F32)
    gq_ref[...] = turned(
        grad_query, cos_ref[...], low_ref[...], high_ref[...], -1.0
    ).astype(BF16)
    grad_key = jnp.concatenate(gk, axis=1) * 0.125
    gkv_ref[0] = turned(
        grad_key, cos_all_ref[...], low_all_ref[...], high_all_ref[...], -1.0
    ).astype(BF16)
    gkv_ref[1] = jnp.concatenate(gv, axis=1).astype(BF16)


def attend_back(query, key_values, grad_mixed, stats, own_tables, all_tables, places_all, places_own):
    rows, total = query.shape[0], key_values.shape[1]
    table = pl.BlockSpec((rows, 128), lambda h: (0, 0))
    table_all = pl.BlockSpec((total, 128), lambda h: (0, 0))
    block = pl.BlockSpec((rows, 128), lambda h: (0, h))
    both = pl.BlockSpec((2, total, 128), lambda h: (0, 0, h))
    return pl.pallas_call(
        attend_back_kernel,
        grid=(PAIRS,),
        in_specs=[
            block, both, block, pl.BlockSpec((1, 2, rows), lambda h: (h, 0, 0)),
            table, table, table, table_all, table_all, table_all,
            pl.BlockSpec((total, 1), lambda h: (0, 0)),
            pl.BlockSpec((1, rows), lambda h: (0, 0)),
        ],
        out_specs=[block, both],
        out_shape=[
            jax.ShapeDtypeStruct((rows, D), BF16),
            jax.ShapeDtypeStruct((2, total, D), BF16),
        ],
        compiler_params=pltpu.CompilerParams(vmem_limit_bytes=VMEM_LIMIT),
        name="attend_back",
        cost_estimate=pl.CostEstimate(
            flops=10 * rows * total * D * 2, bytes_accessed=12 * total * D, transcendentals=rows * total * H
        ),
    )(
        query, key_values, grad_mixed, stats, *own_tables, *all_tables,
        places_all[:, None], places_own[None, :],
    )


def layer_forward(current, weights, geometry):
    (w_qkv, b_qkv, w_out, b_out, w_up, b_up, w_down, b_down, gain_a, shift_a, gain_m, shift_m) = weights
    own_tables, all_tables, places_all, places_own = geometry
    center = current - jnp.mean(current, axis=-1, keepdims=True)
    scale = lax.rsqrt(jnp.mean(center * center, axis=-1, keepdims=True) + EPSILON)
    normal = center * scale
    normed_a = (normal * gain_a + shift_a).astype(BF16)
    normed_m = (normal * gain_m + shift_m).astype(BF16)
    projected_kv = dot(normed_a, w_qkv[:, D:]) + b_qkv[D:]
    own_kv = rotate_keys(projected_kv, own_tables)
    key_values = lax.all_gather(own_kv, "ctx", axis=1, tiled=True)
    projected_q = dot(normed_a, w_qkv[:, :D]) + b_qkv[:D]
    pre = dot(normed_m, w_up) + b_up
    active = (pre * (1.0 + lax.erf(pre * F32(math.sqrt(0.5)))) * 0.5).astype(BF16)
    mlp_branch = dot(active, w_down) + b_down
    mixed, query, stats = attend(projected_q, key_values, own_tables, places_all, places_own)
    attn_branch = dot(mixed, w_out) + b_out
    result = (current + attn_branch + mlp_branch).astype(BF16)
    return result, (normal, scale, normed_a, normed_m, query, key_values, stats, mixed, pre, active)


def layer_backward(weights, geometry, grad_low, kept):
    (w_qkv, b_qkv, w_out, b_out, w_up, b_up, w_down, b_down, gain_a, shift_a, gain_m, shift_m) = weights
    own_tables, all_tables, places_all, places_own = geometry
    normal, scale, normed_a, normed_m, query, key_values, stats, mixed, pre, active = kept
    grad_out = grad_low.astype(F32)
    grad_mixed = dot_t(grad_low, w_out).astype(BF16)
    grad_q, grad_kv_all = attend_back(
        query, key_values, grad_mixed, stats, own_tables, all_tables, places_all, places_own
    )
    grad_kv = lax.psum_scatter(grad_kv_all, "ctx", scatter_dimension=1, tiled=True)
    grad_active = dot_t(grad_low, w_down)
    slope = 0.5 * (1.0 + lax.erf(pre * F32(math.sqrt(0.5)))) + pre * jnp.exp(
        -0.5 * pre * pre
    ) * F32(1.0 / math.sqrt(2.0 * math.pi))
    grad_pre = (grad_active * slope).astype(BF16)
    grad_normed_m = dot_t(grad_pre, w_up)
    grad_projected = jnp.concatenate([grad_q, grad_kv[0], grad_kv[1]], axis=1)
    grad_normed_a = dot_t(grad_projected, w_qkv)
    through = grad_normed_a * gain_a + grad_normed_m * gain_m
    grad_input = (
        grad_out
        + scale
        * (
            through
            - jnp.mean(through, axis=-1, keepdims=True)
            - normal * jnp.mean(through * normal, axis=-1, keepdims=True)
        )
    ).astype(BF16)
    pairs = (
        (normed_a, grad_projected),
        (mixed, grad_low),
        (normed_m, grad_pre),
        (active, grad_low),
    )
    sums = (
        jnp.sum(grad_projected.astype(F32), axis=0),
        jnp.sum(grad_out, axis=0),
        jnp.sum(grad_pre.astype(F32), axis=0),
        jnp.sum(grad_normed_a * normal, axis=0),
        jnp.sum(grad_normed_a, axis=0),
        jnp.sum(grad_normed_m * normal, axis=0),
        jnp.sum(grad_normed_m, axis=0),
    )
    return grad_input, pairs, sums


def half_of(wide, index):
    width = wide.shape[1] // 2
    return lax.dynamic_slice_in_dim(wide, index * width, width, 1)


def weight_terms(pairs, section):
    done = []
    for left, right in pairs:
        left_both = jnp.concatenate([left, swapped(left)], axis=0)
        right_both = jnp.concatenate(
            [half_of(right, section), swapped(half_of(right, 1 - section))], axis=0
        )
        done.append(t_dot(left_both, right_both).astype(BF16))
    return done


def folded(tall, chunks):
    rows, width = tall.shape[0] // (4 * chunks), tall.shape[1]
    blocks = tall.reshape(chunks, 4, rows, width)
    return jnp.transpose(blocks, (0, 2, 1, 3)).reshape(chunks * rows, 4 * width)


def unfolded(flat, chunks):
    rows, width = flat.shape[0] // chunks, flat.shape[1] // 4
    blocks = flat.reshape(chunks, rows, 4, width)
    return jnp.transpose(blocks, (0, 2, 1, 3)).reshape(chunks * 4 * rows, width)


def padded(thin):
    return jnp.pad(thin, ((0, 0), (0, 128 - thin.shape[1])))


def per_device(
    tokens, cotangent, block_map, w_qkv, b_qkv, w_out, b_out, w_up, b_up, w_down, b_down,
    gain_attn, shift_attn, gain_mlp, shift_mlp,
):
    section = lax.axis_index("section")
    first = section == 0
    ctx_count = lax.axis_size("ctx")
    shards_n = lax.axis_size("wshard")
    rows = tokens.shape[1]

    def pick(stacked):
        return lax.dynamic_index_in_dim(stacked, section, 0, keepdims=False)

    own_tokens, own_cotangent, order_row = pick(tokens), pick(cotangent), pick(block_map)
    block_rows = rows * ctx_count // order_row.shape[0]
    places_all = positions(order_row, block_rows)
    start = lax.axis_index("ctx") * rows
    all_tables = turn_tables(places_all)
    places_own = lax.dynamic_slice_in_dim(places_all, start, rows, 0)
    own_tables = tuple(lax.dynamic_slice_in_dim(table, start, rows, 0) for table in all_tables)
    geometry = (own_tables, all_tables, places_all, places_own)

    small = (b_qkv, b_out, b_up, b_down, gain_attn, shift_attn, gain_mlp, shift_mlp)
    widths = [vector.shape[1] for vector in small]
    part_rows = w_qkv.shape[1] // ctx_count
    chunks = shards_n * ctx_count
    thin_width = sum(widths) // w_qkv.shape[1]

    def part_of(shard):
        count = shard.shape[0] // ctx_count
        return lax.dynamic_slice_in_dim(shard, lax.axis_index("ctx") * count, count, 0)

    def gathered(parts):
        joined = jnp.concatenate(parts, axis=1)
        return lax.all_gather(joined, ("section", "wshard", "ctx"), axis=0, tiled=True).reshape(
            2, chunks * part_rows, -1
        )

    vector_rows = part_of(jnp.concatenate(small, axis=1)[0].reshape(-1, thin_width))
    both_a = gathered([part_of(w_qkv[0]), part_of(w_out[0]), padded(vector_rows)])
    both_b = gathered([part_of(w_up[0]), folded(part_of(w_down[0]), 1)])
    packed = both_a[:, :, 4 * D : 4 * D + thin_width].reshape(2, shards_n, -1)
    vectors, at = [], 0
    for width in widths:
        vectors.append(packed[:, :, at : at + width].reshape(2, -1).astype(F32))
        at += width

    def layer_weights(j):
        qkv, out = both_a[j, :, : 3 * D], both_a[j, :, 3 * D : 4 * D]
        up, down = both_b[j, :, :FF], unfolded(both_b[j, :, FF:], chunks)
        (v_qkv, v_out, v_up, v_down, g_a, s_a, g_m, s_m) = (vector[j] for vector in vectors)
        return (qkv, v_qkv, out, v_out, up, v_up, down, v_down, g_a, s_a, g_m, s_m)

    lower, upper = layer_weights(0), layer_weights(1)
    middle, kept_lower = layer_forward(own_tokens.astype(F32), lower, geometry)
    final, kept_upper = layer_forward(middle.astype(F32), upper, geometry)
    grad_middle, pairs_upper, sums_upper = layer_backward(upper, geometry, own_cotangent, kept_upper)
    upper_terms = weight_terms(pairs_upper, section)
    grad_input, pairs_lower, sums_lower = layer_backward(lower, geometry, grad_middle, kept_lower)
    lower_terms = weight_terms(pairs_lower, section)

    def together(low_part, high_part):
        own = jnp.where(first, low_part, high_part)
        other = swapped(jnp.where(first, high_part, low_part))
        return jnp.where(first, own, other), jnp.where(first, other, own)

    outputs = jnp.stack(together(middle, final))[None]
    boundary = jnp.stack(together(grad_input, grad_middle))[None].astype(F32)

    def packed_terms(terms, sums):
        t_qkv, t_out, t_up, t_down = terms
        g_qkv, g_bias, g_up, g_ga, g_sa, g_gm, g_sm = (part.reshape(shards_n, -1) for part in sums)
        shard_sums = jnp.concatenate([g_qkv, g_bias, g_up, g_bias, g_ga, g_sa, g_gm, g_sm], axis=1)
        thin = padded(shard_sums.astype(BF16).reshape(-1, thin_width))
        return [t_qkv, t_out, t_up, folded(t_down, chunks), thin]

    everything = jnp.concatenate(
        packed_terms(lower_terms, sums_lower) + packed_terms(upper_terms, sums_upper), axis=1
    )
    summed = lax.psum_scatter(everything, ("wshard", "ctx"), scatter_dimension=0, tiled=True)
    low_part, high_part = jnp.split(summed, 2, axis=1)
    own = jnp.where(first, low_part, high_part)
    other = swapped(jnp.where(first, high_part, low_part))
    left, right = jnp.where(first, own, other), jnp.where(first, other, own)
    cuts = [(0, 3 * D // 2), (3 * D // 2, 2 * D), (2 * D, 2 * D + FF // 2)]
    columns = [piece[:, lo:hi] for lo, hi in cuts for piece in (left, right)]
    base = 2 * D + FF // 2
    for k in range(4):
        at = base + k * (D // 2)
        columns += [left[:, at : at + D // 2], right[:, at : at + D // 2]]
    at = base + 2 * D
    columns.append((left[:, at:].astype(F32) + right[:, at:].astype(F32)).astype(BF16))
    shard = lax.all_gather(jnp.concatenate(columns, axis=1), "ctx", axis=0, tiled=True).astype(F32)
    ends = [0, 3 * D, 4 * D, 4 * D + FF]
    grads = [shard[:, lo:hi][None] for lo, hi in zip(ends[:-1], ends[1:])]
    at = 4 * D + FF
    grads.append(unfolded(shard[:, at : at + 4 * D], ctx_count)[None])
    at += 4 * D
    own_sums = shard[:, at : at + thin_width].reshape(1, -1)
    vector_grads, at = [], 0
    for width in widths:
        vector_grads.append(own_sums[:, at : at + width])
        at += width
    s_qkv, s_out, s_up, s_down, s_ga, s_sa, s_gm, s_sm = vector_grads
    return (
        outputs, boundary, grads[0], s_qkv, grads[1], s_out, grads[2], s_up, grads[3], s_down,
        s_ga, s_sa, s_gm, s_sm,
    )


def solution(mesh):
    wide = P("section", "wshard", None)
    thin = P("section", "wshard")
    rows = P("wshard", "ctx", None)
    stacked = P("section", "wshard", "ctx", None)
    weights = (wide, thin) * 4 + (thin,) * 4
    return jax.shard_map(
        per_device, mesh=mesh, in_specs=(rows, rows, P("wshard", None)) + weights,
        out_specs=(stacked, stacked) + weights, check_vma=False,
    )
```
